128 devices in a mesh: example: 16 (over x, z_hi, core), proj: 8 (over z_lo, y).
Axes of the slice: x: 4, y: 4, z: 4 (z_hi: 2, z_lo: 2; z = z_hi * 2 + z_lo), core: 2. Of those that a mesh axis runs over, the one named last changes fastest.
Arguments:
- queries: bfloat16 [512, 131072], P('example', 'proj'), may hold values from -6 to 6
- store: bfloat16 [12288, 131072], P('example', 'proj'), may hold values from -6 to 6
- block_scale: float32 [12288, 1024], P('example', 'proj'), may hold values from 0.1 to 10
- query_inv: float32 [512], replicated, may hold values from 0.01 to 0.1
- train_inv: float32 [12288], P('example'), may hold values from 0.01 to 0.1
Outputs:
- scores: float32 [512, 12288], P('proj', 'example')
The draws below stay inside these ranges and needn't reach their ends.
All inputs are finite; a program needn't handle non-finite values.
Results may differ from the reference program's by a relative error of at most 0.0029.
Values may be sent and summed in bfloat16 or wider, within the bound.
A program may use at most 192 MiB of HBM per device.

```python
import math
import jax
import jax.numpy as jnp
from jax import lax

P_SIZE = 131072
BLOCK = 128
ROWS_DEV = 768
TRAIN = 12288
Q = 512
N_EXAMPLE = 16


def spiked(result, stream_key, source, target, parts, factor):
    owner, partner = [(jnp.arange(result.shape[axis_at]) // (result.shape[axis_at] // parts)).reshape([-1 if axis == axis_at else 1 for axis in range(result.ndim)]) for axis_at in (source, target)]
    chosen = jax.random.permutation(stream_key, parts)[partner]
    strong = (owner == chosen) | (owner == (partner + parts // 2) % parts)
    return jnp.where(strong, factor * result, result)


def level_of(stream_key, dims, split, smallest, high):
    def one(axis_at, parts):
        draws = jax.random.uniform(jax.random.fold_in(jax.random.fold_in(stream_key, 6), axis_at), (parts,), jnp.float32, smallest / len(split), high / len(split))
        return jnp.repeat(jnp.exp(draws), dims[axis_at] // parts).reshape((-1,) + (1,) * (len(dims) - axis_at - 1))

    factor_of = one(*split[0])
    for cut in split[1:]:
        factor_of = factor_of * one(*cut)
    return factor_of


def scatter_about(rng, dims, spread, bound, cuts=(), held_as=jnp.bfloat16):
    drawn = jax.random.normal(rng, dims, jnp.float32) * spread
    if len(cuts) > 0:
        drawn = level_of(rng, dims, cuts, -0.22, 0.18) * drawn
    return jnp.clip(drawn, min=-bound, max=bound).astype(held_as)


def bell_draw_with(key, dims, spread, limit, pieces, heavy, dtype=jnp.bfloat16):
    array = spread * jax.random.normal(key, dims, jnp.float32)
    if pieces:
        array = array * level_of(key, dims, pieces, -0.22, 0.18)
    return jnp.clip(spiked(array, jax.random.fold_in(key, 3), *heavy), -limit, limit).astype(dtype)


def setup_inputs(seed: int = 0) -> dict:
    key_list = jax.random.split(jax.random.key(seed), 6)
    queries = bell_draw_with(key_list[0], (Q, P_SIZE), 1.0, 6.0, ((0, 16), (1, 8)), (1, 0, 16, 2.0))
    store = scatter_about(key_list[1], (TRAIN, P_SIZE), 1.0, 6.0, ((0, 16), (1, 8)))
    block_scale = jnp.clip(jnp.exp(math.log(10.0) - 4.6051702 * jax.random.uniform(key_list[2], (TRAIN, P_SIZE // BLOCK), jnp.float32) ** level_of(key_list[2], (TRAIN, P_SIZE // BLOCK), ((0, 16), (1, 8)), -0.2, 0.2)), 0.1, 10.0)
    query_inv = jnp.clip(jnp.exp(jax.random.uniform(key_list[3], (Q,), jnp.float32, math.log(0.01), math.log(0.1))), 0.01, 0.1)
    train_inv = jnp.clip(jnp.exp(math.log(0.1) - 2.3025851 * jax.random.uniform(key_list[4], (TRAIN,), jnp.float32) ** level_of(key_list[4], (TRAIN,), ((0, 16),), -0.2, 0.2)), 0.01, 0.1)
    return dict(queries=queries, store=store, block_scale=block_scale, query_inv=query_inv, train_inv=train_inv)


def reference(queries, store, block_scale, query_inv, train_inv):
    blocks = store.reshape(N_EXAMPLE, ROWS_DEV, P_SIZE)
    scale_blocks = block_scale.reshape(N_EXAMPLE, ROWS_DEV, P_SIZE // BLOCK)

    def one_block(pair):
        stored, scales = pair
        dequant = (stored.astype(jnp.float32).reshape(ROWS_DEV, P_SIZE // BLOCK, BLOCK) * scales[:, :, None]).reshape(ROWS_DEV, P_SIZE).astype(jnp.bfloat16)
        return jnp.dot(queries, dequant.T, preferred_element_type=jnp.float32)

    raw_scores = lax.map(one_block, (blocks, scale_blocks))
    raw_scores = jnp.transpose(raw_scores, (1, 0, 2)).reshape(Q, TRAIN)
    return raw_scores * query_inv[:, None] * train_inv[None, :]
```

```python
import functools

import jax
import jax.numpy as jnp
from jax import lax
from jax.experimental import pallas as pl
from jax.experimental.pallas import tpu as pltpu
from jax.sharding import PartitionSpec as P

BF = jnp.bfloat16
F32 = jnp.float32
MESH = pl.DeviceIdType.MESH
NT = (((1,), (1,)), ((), ()))
STRIP = 16
PIECES = 16
WIDE = 8
AHEAD = 3
LAG = 3
B, F, Z, X2, ZB, ZF, ZX2 = range(7)


def kernel(
    q_hbm, s_hbm, scale_hbm, qinv_ref, tinv_ref, o_ref,
    qbuf, g, st, sc, acc, got,
    in_sem, st_sem, ici_sem, sib_sem, own_sem, out_sem, own_out, rs_sem, rs_out,
):
    rows, width = g.shape
    piece_w = width // WIDE
    half = width // 2
    e = lax.axis_index("example")
    p = lax.axis_index("proj")
    c = lax.rem(e, 2)
    zh = lax.rem(e // 2, 2)
    x = e // 4
    y = lax.rem(p, 4)
    zl = p // 4
    fdir = 1 - 2 * c
    xf = lax.rem(x + fdir + 4, 4)
    xb = lax.rem(x - fdir + 4, 4)
    x2 = lax.rem(x + 2, 4)
    zo = 1 - zh

    def at(x_, zh_, c_):
        return {"example": x_ * 4 + zh_ * 2 + c_, "proj": p}

    sib = at(x, zh, 1 - c)
    front = at(xf, zh, c)
    back = at(xb, zh, c)
    across = at(x, zo, c)
    owners = []
    for dz in range(2):
        for dy in range(4):
            if dz or dy:
                y_, zl_ = lax.rem(y + dy, 4), lax.rem(zl + dz, 2)
                owners.append((dz * 4 + dy - 1, zl_ * 4 + y_))

    def strip_row(h, x_, zh_, c_):
        chip = x_ * 2 + zh_
        return chip * 32 + c_ * 16 if h == 0 else 256 + c_ * 128 + chip * 16

    own_refs = [
        qbuf.at[pl.ds(pl.multiple_of(strip_row(h, x, zh, c), STRIP), STRIP), :]
        for h in range(2)
    ]
    own_in = [
        pltpu.make_async_copy(q_hbm.at[pl.ds(h * STRIP, STRIP), :], own_refs[h], in_sem.at[h])
        for h in range(2)
    ]
    scale_in = pltpu.make_async_copy(scale_hbm, sc, in_sem.at[2])

    def chunk_in(j):
        slot = lax.rem(j, 2)
        cols = pl.ds(pl.multiple_of(j * piece_w, piece_w), piece_w)
        return pltpu.make_async_copy(s_hbm.at[:, cols], st.at[slot], st_sem.at[slot])

    own_in[0].start()
    own_in[1].start()
    scale_in.start()
    chunk_in(0).start()
    chunk_in(1).start()

    barrier = pltpu.get_barrier_semaphore()
    for target in (sib, front, back, across):
        pl.semaphore_signal(barrier, inc=1, device_id=target, device_id_type=MESH)
    for _, owner in owners:
        pl.semaphore_signal(
            barrier, inc=1, device_id={"example": e, "proj": owner}, device_id_type=MESH
        )
    pl.semaphore_wait(barrier, 4 + len(owners))

    def place(n, x_, zh_):
        chip = x_ * 2 + zh_
        first = n < WIDE
        row = jnp.where(first, chip * 32 + c * 16, 256 + (n // 4 - 2) * 128 + chip * 16)
        col = jnp.where(first, n * piece_w, c * half + lax.rem(n, 4) * piece_w)
        return qbuf.at[
            pl.ds(pl.multiple_of(row, STRIP), STRIP),
            pl.ds(pl.multiple_of(col, piece_w), piece_w),
        ]

    def send(n, x_, zh_, target, recv):
        ref = place(n, x_, zh_)
        pltpu.make_async_remote_copy(
            ref, ref, out_sem.at[n], recv, device_id=target, device_id_type=MESH
        ).start()

    def arrived(n, x_, zh_, slot):
        ref = place(n, x_, zh_)
        pltpu.make_async_copy(ref, ref, ici_sem.at[n, slot]).wait()

    def spread_along_z(n):
        return lax.rem(n, 3) == 1

    def send_own(n):
        send(n, x, zh, front, ici_sem.at[n, B])
        send(n, x, zh, back, ici_sem.at[n, F])
        send(n, x, zh, across, ici_sem.at[n, Z])

    def stage1(n):
        along_z = spread_along_z(n)
        arrived(n, xb, zh, B)
        send(n, xb, zh, front, ici_sem.at[n, X2])

        @pl.when(along_z)
        def _():
            send(n, xb, zh, across, ici_sem.at[n, ZB])

        send(n, xb, zh, sib, sib_sem.at[n])
        arrived(n, x, zo, Z)

        @pl.when(jnp.logical_not(along_z))
        def _():
            send(n, x, zo, front, ici_sem.at[n, ZB])
            send(n, x, zo, back, ici_sem.at[n, ZF])

        send(n, x, zo, sib, sib_sem.at[n])
        arrived(n, xf, zh, F)

        @pl.when(along_z)
        def _():
            send(n, xf, zh, across, ici_sem.at[n, ZF])

        send(n, xf, zh, sib, sib_sem.at[n])

    def stage2(n):
        along_z = spread_along_z(n)
        arrived(n, xb, zo, ZB)

        @pl.when(jnp.logical_not(along_z))
        def _():
            send(n, xb, zo, front, ici_sem.at[n, ZX2])

        send(n, xb, zo, sib, sib_sem.at[n])
        arrived(n, x2, zh, X2)

        @pl.when(along_z)
        def _():
            send(n, x2, zh, across, ici_sem.at[n, ZX2])

        send(n, x2, zh, sib, sib_sem.at[n])
        arrived(n, xf, zo, ZF)
        send(n, xf, zo, sib, sib_sem.at[n])

    def stage3(n):
        arrived(n, x2, zo, ZX2)
        send(n, x2, zo, sib, sib_sem.at[n])

    def dequant(j):
        slot = lax.rem(j, 2)
        chunk_in(j).wait()
        blocks = piece_w // 128
        s = pltpu.roll(sc[...], lax.rem(128 - j * blocks, 128), 1)
        for r in range(0, rows, 128):
            for b in range(blocks):
                cols = pl.ds(pl.multiple_of(j * piece_w + b * 128, 128), 128)
                part = st[slot, r : r + 128, b * 128 : (b + 1) * 128].astype(F32)
                g[r : r + 128, cols] = (part * s[r : r + 128, b : b + 1]).astype(BF)

        @pl.when(j + 2 < WIDE)
        def _():
            chunk_in(j + 2).start()

    def multiply(n):
        pieces = qbuf.at[0 : 7 * STRIP, 0:piece_w]
        pltpu.make_async_copy(pieces, pieces, sib_sem.at[n]).wait()

        @pl.when(n < WIDE)
        def _():
            cols = pl.ds(pl.multiple_of(n * piece_w, piece_w), piece_w)
            acc[0:256, :] += lax.dot_general(
                qbuf[0:256, cols], g[:, cols], NT, preferred_element_type=F32
            )

        @pl.when(n >= WIDE)
        def _():
            at_row = pl.ds(pl.multiple_of(256 + (n // 4 - 2) * 128, 128), 128)
            for k in range(2):
                col = k * half + lax.rem(n, 4) * piece_w
                cols = pl.ds(pl.multiple_of(col, piece_w), piece_w)
                acc[at_row, :] += lax.dot_general(
                    qbuf[at_row, cols], g[:, cols], NT, preferred_element_type=F32
                )

    first_row, count, landing = (0, 256, 384), (32, 16, 16), (0, 32, 48)

    def send_sums(k):
        for slot, owner in owners:
            start = pl.multiple_of(first_row[k] + owner * count[k], STRIP)
            pltpu.make_async_remote_copy(
                acc.at[pl.ds(start, count[k]), :],
                got.at[slot, pl.ds(landing[k], count[k]), :],
                rs_out.at[k],
                rs_sem.at[k, slot],
                device_id={"example": e, "proj": owner},
                device_id_type=MESH,
            ).start()

    lane = lax.broadcasted_iota(jnp.int32, (64, qinv_ref.shape[0]), 1)
    row = lax.broadcasted_iota(jnp.int32, (64, qinv_ref.shape[0]), 0)
    qrow = qinv_ref[...].reshape(1, -1)
    qcol = jnp.sum(jnp.where(lane == row + p * 64, qrow, 0.0), axis=1, keepdims=True)
    trow = tinv_ref[...].reshape(1, -1)

    def finish(k):
        start = pl.multiple_of(first_row[k] + p * count[k], STRIP)
        total = acc[pl.ds(start, count[k]), :]
        for slot in range(7):
            ref = got.at[slot, pl.ds(landing[k], count[k]), :]
            pltpu.make_async_copy(ref, ref, rs_sem.at[k, slot]).wait()
            total += got[slot, landing[k] : landing[k] + count[k], :]
        pieces = [(0, 0), (16, 32)] if k == 0 else [(0, 16 if k == 1 else 48)]
        for here, there in pieces:
            o_ref[there : there + 16, :] = (
                total[here : here + 16, :] * qcol[there : there + 16, :] * trow
            )

    own_in[0].wait()
    own_in[1].wait()
    for h in range(2):
        if h == 1:
            for n in range(AHEAD):
                send_own(n)
        pltpu.make_async_remote_copy(
            own_refs[h], own_refs[h], own_out.at[h], own_sem.at[h],
            device_id=sib, device_id_type=MESH,
        ).start()
    acc[...] = jnp.zeros_like(acc)
    scale_in.wait()
    dequant(0)
    for h in range(2):
        ref = qbuf.at[pl.ds(pl.multiple_of(strip_row(h, x, zh, 1 - c), STRIP), STRIP), :]
        pltpu.make_async_copy(ref, ref, own_sem.at[h]).wait()

    def step(s, carry):
        @pl.when(s + AHEAD < PIECES)
        def _():
            send_own(s + AHEAD)

        @pl.when(s < PIECES)
        def _():
            stage1(s)

        @pl.when(s + 1 < WIDE)
        def _():
            dequant(s + 1)

        @pl.when((s >= 1) & (s < PIECES + 1))
        def _():
            stage2(s - 1)

        @pl.when((s >= 2) & (s < PIECES + 2))
        def _():
            stage3(s - 2)

        @pl.when(s >= LAG)
        def _():
            multiply(s - LAG)

        @pl.when(s == WIDE - 1 + LAG)
        def _():
            send_sums(0)

        @pl.when(s == WIDE + 3 + LAG)
        def _():
            send_sums(1)

        return carry

    lax.fori_loop(0, PIECES + LAG, step, 0)
    send_sums(2)
    finish(0)
    finish(1)
    finish(2)
    for n in range(PIECES):
        pieces = qbuf.at[0 : 14 * STRIP, 0:piece_w]
        pltpu.make_async_copy(pieces, pieces, out_sem.at[n]).wait()
    for h in range(2):
        pltpu.make_async_copy(own_refs[h], own_refs[h], own_out.at[h]).wait()
    for k in range(3):
        ref = acc.at[0 : 7 * count[k], :]
        pltpu.make_async_copy(ref, ref, rs_out.at[k]).wait()


def body(queries, store, block_scale, query_inv, train_inv):
    rows, width = store.shape
    n_query = query_inv.shape[0]
    hbm = pl.BlockSpec(memory_space=pl.ANY)
    vmem = pl.BlockSpec(memory_space=pltpu.VMEM)
    dma = pltpu.SemaphoreType.DMA
    return pl.pallas_call(
        kernel,
        out_shape=jax.ShapeDtypeStruct((n_query // 8, rows), F32),
        in_specs=[hbm, hbm, hbm, vmem, vmem],
        out_specs=vmem,
        scratch_shapes=[
            pltpu.VMEM((n_query, width), BF),
            pltpu.VMEM((rows, width), BF),
            pltpu.VMEM((2, rows, width // WIDE), BF),
            pltpu.VMEM((rows, width // 128), F32),
            pltpu.VMEM((n_query, rows), F32),
            pltpu.VMEM((7, n_query // 8, rows), F32),
            dma((3,)),
            dma((2,)),
            dma((PIECES, 7)),
            dma((PIECES,)),
            dma((2,)),
            dma((PIECES,)),
            dma((2,)),
            dma((3, 7)),
            dma((3,)),
        ],
        compiler_params=pltpu.CompilerParams(
            collective_id=0, has_side_effects=True, vmem_limit_bytes=60 << 20
        ),
        cost_estimate=pl.CostEstimate(
            flops=2 * n_query * rows * width,
            bytes_accessed=2 * rows * width,
            transcendentals=0,
        ),
        name="gather_score",
    )(queries, store, block_scale, query_inv, train_inv)


def solution(mesh):
    placed = (P("example", "proj"), P("example", "proj"), P("example", "proj"), P(), P("example"))
    return jax.shard_map(
        body, mesh=mesh, in_specs=placed, out_specs=P("proj", "example"), check_vma=False
    )
```

```python
import functools

import jax
import jax.numpy as jnp
from jax import lax
from jax.experimental import pallas as pl
from jax.experimental.pallas import tpu as pltpu
from jax.sharding import PartitionSpec as P

BF = jnp.bfloat16
F32 = jnp.float32
MESH = pl.DeviceIdType.MESH
NT = (((1,), (1,)), ((), ()))
STRIP = 16
WIDE = 8
PIECES = 2 * WIDE
AHEAD = 4
LAG2 = 4
LAG3 = 8
LAG = 9
B, F, Z, X2, ZB, ZF, ZX2 = range(7)


def kernel(
    q_hbm, s_hbm, scale_hbm, qinv_ref, tinv_ref, o_ref,
    qbuf, g, st, sc, acc, sums, got,
    in_sem, st_sem, ici_sem, sib_sem, own_sem, out_sem, own_out, rs_sem, rs_out,
):
    rows, width = g.shape
    piece_w = width // WIDE
    e = lax.axis_index("example")
    p = lax.axis_index("proj")
    c = lax.rem(e, 2)
    zh = lax.rem(e // 2, 2)
    x = e // 4
    y = lax.rem(p, 4)
    zl = p // 4
    fdir = 1 - 2 * c
    xf = lax.rem(x + fdir + 4, 4)
    xb = lax.rem(x - fdir + 4, 4)
    x2 = lax.rem(x + 2, 4)
    zo = 1 - zh

    def at(x_, zh_, c_):
        return {"example": x_ * 4 + zh_ * 2 + c_, "proj": p}

    sib = at(x, zh, 1 - c)
    front = at(xf, zh, c)
    back = at(xb, zh, c)
    across = at(x, zo, c)
    owners = []
    for dz in range(2):
        for dy in range(4):
            if dz or dy:
                y_, zl_ = lax.rem(y + dy, 4), lax.rem(zl + dz, 2)
                owners.append((dz * 4 + dy - 1, zl_ * 4 + y_))

    def strip_row(h, x_, zh_, c_):
        return h * 256 + (x_ * 2 + zh_) * 32 + c_ * STRIP

    own_refs = [
        qbuf.at[pl.ds(pl.multiple_of(strip_row(h, x, zh, c), STRIP), STRIP), :]
        for h in range(2)
    ]
    own_in = [
        pltpu.make_async_copy(q_hbm.at[pl.ds(h * STRIP, STRIP), :], own_refs[h], in_sem.at[h])
        for h in range(2)
    ]
    scale_in = pltpu.make_async_copy(scale_hbm, sc, in_sem.at[2])

    def chunk_in(j):
        slot = lax.rem(j, 2)
        cols = pl.ds(pl.multiple_of(j * piece_w, piece_w), piece_w)
        return pltpu.make_async_copy(s_hbm.at[:, cols], st.at[slot], st_sem.at[slot])

    own_in[0].start()
    own_in[1].start()
    scale_in.start()
    chunk_in(0).start()
    chunk_in(1).start()

    barrier = pltpu.get_barrier_semaphore()
    for target in (sib, front, back, across):
        pl.semaphore_signal(barrier, inc=1, device_id=target, device_id_type=MESH)
    for _, owner in owners:
        pl.semaphore_signal(
            barrier, inc=1, device_id={"example": e, "proj": owner}, device_id_type=MESH
        )
    pl.semaphore_wait(barrier, 4 + len(owners))

    def place(n, x_, zh_):
        chip = x_ * 2 + zh_
        row = (n // WIDE) * 256 + chip * 32 + c * STRIP
        col = lax.rem(n, WIDE) * piece_w
        return qbuf.at[
            pl.ds(pl.multiple_of(row, STRIP), STRIP),
            pl.ds(pl.multiple_of(col, piece_w), piece_w),
        ]

    def send(n, x_, zh_, target, recv):
        ref = place(n, x_, zh_)
        pltpu.make_async_remote_copy(
            ref, ref, out_sem.at[n], recv, device_id=target, device_id_type=MESH
        ).start()

    def arrived(n, x_, zh_, slot):
        ref = place(n, x_, zh_)
        pltpu.make_async_copy(ref, ref, ici_sem.at[n, slot]).wait()

    def spread_along_z(n):
        return (lax.rem(n + 2 * c, 5) == 1) | (lax.rem(n + 2 * c, 5) == 3)

    def send_own(n):
        send(n, x, zh, across, ici_sem.at[n, Z])
        send(n, x, zh, front, ici_sem.at[n, B])
        send(n, x, zh, back, ici_sem.at[n, F])

    def stage1(n):
        along_z = spread_along_z(n)
        arrived(n, xb, zh, B)
        send(n, xb, zh, front, ici_sem.at[n, X2])

        @pl.when(along_z)
        def _():
            send(n, xb, zh, across, ici_sem.at[n, ZB])

        send(n, xb, zh, sib, sib_sem.at[n])
        arrived(n, x, zo, Z)

        @pl.when(jnp.logical_not(along_z))
        def _():
            send(n, x, zo, front, ici_sem.at[n, ZB])
            send(n, x, zo, back, ici_sem.at[n, ZF])

        send(n, x, zo, sib, sib_sem.at[n])
        arrived(n, xf, zh, F)

        @pl.when(along_z)
        def _():
            send(n, xf, zh, across, ici_sem.at[n, ZF])

        send(n, xf, zh, sib, sib_sem.at[n])

    def stage2(n):
        along_z = spread_along_z(n)
        arrived(n, xb, zo, ZB)

        @pl.when(jnp.logical_not(along_z))
        def _():
            send(n, xb, zo, front, ici_sem.at[n, ZX2])

        send(n, xb, zo, sib, sib_sem.at[n])
        arrived(n, x2, zh, X2)

        @pl.when(along_z)
        def _():
            send(n, x2, zh, across, ici_sem.at[n, ZX2])

        send(n, x2, zh, sib, sib_sem.at[n])
        arrived(n, xf, zo, ZF)
        send(n, xf, zo, sib, sib_sem.at[n])

    def stage3(n):
        arrived(n, x2, zo, ZX2)
        send(n, x2, zo, sib, sib_sem.at[n])

    def dequant(j):
        slot = lax.rem(j, 2)
        chunk_in(j).wait()
        blocks = piece_w // 128
        s = pltpu.roll(sc[...], lax.rem(128 - j * blocks, 128), 1)
        for r in range(0, rows, 128):
            for b in range(blocks):
                cols = pl.ds(pl.multiple_of(j * piece_w + b * 128, 128), 128)
                part = st[slot, r : r + 128, b * 128 : (b + 1) * 128].astype(F32)
                g[r : r + 128, cols] = (part * s[r : r + 128, b : b + 1]).astype(BF)

        @pl.when(j + 2 < WIDE)
        def _():
            chunk_in(j + 2).start()

    def multiply(n):
        pieces = qbuf.at[0 : 7 * STRIP, 0:piece_w]
        pltpu.make_async_copy(pieces, pieces, sib_sem.at[n]).wait()

        group = pl.ds(pl.multiple_of(n // WIDE * 256, 256), 256)
        cols = pl.ds(pl.multiple_of(lax.rem(n, WIDE) * piece_w, piece_w), piece_w)
        acc[group, :] += lax.dot_general(
            qbuf[group, cols], g[:, cols], NT, preferred_element_type=F32
        )

    first_row, count, landing = (0, 256), (32, 32), (0, 32)

    def send_sums(k):
        group = pl.ds(first_row[k], 8 * count[k])
        sums[group, :] = acc[group, :].astype(BF)
        for slot, owner in owners:
            start = pl.multiple_of(first_row[k] + owner * count[k], STRIP)
            pltpu.make_async_remote_copy(
                sums.at[pl.ds(start, count[k]), :],
                got.at[slot, pl.ds(landing[k], count[k]), :],
                rs_out.at[k],
                rs_sem.at[k, slot],
                device_id={"example": e, "proj": owner},
                device_id_type=MESH,
            ).start()

    lane = lax.broadcasted_iota(jnp.int32, (64, qinv_ref.shape[0]), 1)
    row = lax.broadcasted_iota(jnp.int32, (64, qinv_ref.shape[0]), 0)
    qrow = qinv_ref[...].reshape(1, -1)
    qcol = jnp.sum(jnp.where(lane == row + p * 64, qrow, 0.0), axis=1, keepdims=True)
    trow = tinv_ref[...].reshape(1, -1)

    def finish(k):
        start = pl.multiple_of(first_row[k] + p * count[k], STRIP)
        total = acc[pl.ds(start, count[k]), :]
        for slot in range(7):
            ref = got.at[slot, pl.ds(landing[k], count[k]), :]
            pltpu.make_async_copy(ref, ref, rs_sem.at[k, slot]).wait()
            total += got[slot, landing[k] : landing[k] + count[k], :].astype(F32)
        for here, there in ((0, 16 * k), (16, 32 + 16 * k)):
            o_ref[there : there + 16, :] = (
                total[here : here + 16, :] * qcol[there : there + 16, :] * trow
            )

    own_in[0].wait()
    own_in[1].wait()
    for h in range(2):
        if h == 1:
            for n in range(AHEAD):
                send_own(n)
        pltpu.make_async_remote_copy(
            own_refs[h], own_refs[h], own_out.at[h], own_sem.at[h],
            device_id=sib, device_id_type=MESH,
        ).start()
    acc[...] = jnp.zeros_like(acc)
    scale_in.wait()
    dequant(0)
    for h in range(2):
        ref = qbuf.at[pl.ds(pl.multiple_of(strip_row(h, x, zh, 1 - c), STRIP), STRIP), :]
        pltpu.make_async_copy(ref, ref, own_sem.at[h]).wait()

    def step(s, carry):
        @pl.when(s + AHEAD < PIECES)
        def _():
            send_own(s + AHEAD)

        @pl.when((s >= LAG3) & (s < PIECES + LAG3))
        def _():
            stage3(s - LAG3)

        @pl.when((s >= LAG2) & (s < PIECES + LAG2))
        def _():
            stage2(s - LAG2)

        @pl.when(s < PIECES)
        def _():
            stage1(s)

        @pl.when(s + 1 < WIDE)
        def _():
            dequant(s + 1)

        @pl.when(s >= LAG)
        def _():
            multiply(s - LAG)

        @pl.when(s == WIDE - 1 + LAG)
        def _():
            send_sums(0)

        return carry

    lax.fori_loop(0, PIECES + LAG, step, 0)
    send_sums(1)
    finish(0)
    finish(1)
    for n in range(PIECES):
        pieces = qbuf.at[0 : 14 * STRIP, 0:piece_w]
        pltpu.make_async_copy(pieces, pieces, out_sem.at[n]).wait()
    for h in range(2):
        pltpu.make_async_copy(own_refs[h], own_refs[h], own_out.at[h]).wait()
    for k in range(2):
        ref = sums.at[0 : 7 * count[k], :]
        pltpu.make_async_copy(ref, ref, rs_out.at[k]).wait()


def body(queries, store, block_scale, query_inv, train_inv):
    rows, width = store.shape
    n_query = query_inv.shape[0]
    hbm = pl.BlockSpec(memory_space=pl.ANY)
    vmem = pl.BlockSpec(memory_space=pltpu.VMEM)
    dma = pltpu.SemaphoreType.DMA
    return pl.pallas_call(
        kernel,
        out_shape=jax.ShapeDtypeStruct((n_query // 8, rows), F32),
        in_specs=[hbm, hbm, hbm, vmem, vmem],
        out_specs=vmem,
        scratch_shapes=[
            pltpu.VMEM((n_query, width), BF),
            pltpu.VMEM((rows, width), BF),
            pltpu.VMEM((2, rows, width // WIDE), BF),
            pltpu.VMEM((rows, width // 128), F32),
            pltpu.VMEM((n_query, rows), F32),
            pltpu.VMEM((n_query, rows), BF),
            pltpu.VMEM((7, n_query // 8, rows), BF),
            dma((3,)),
            dma((2,)),
            dma((PIECES, 7)),
            dma((PIECES,)),
            dma((2,)),
            dma((PIECES,)),
            dma((2,)),
            dma((2, 7)),
            dma((2,)),
        ],
        compiler_params=pltpu.CompilerParams(
            collective_id=0, has_side_effects=True, vmem_limit_bytes=60 << 20
        ),
        cost_estimate=pl.CostEstimate(
            flops=2 * n_query * rows * width,
            bytes_accessed=2 * rows * width,
            transcendentals=0,
        ),
        name="gather_score",
    )(queries, store, block_scale, query_inv, train_inv)


def solution(mesh):
    placed = (P("example", "proj"), P("example", "proj"), P("example", "proj"), P(), P("example"))
    return jax.shard_map(
        body, mesh=mesh, in_specs=placed, out_specs=P("proj", "example"), check_vma=False
    )
```

```python
import functools

import jax
import jax.numpy as jnp
from jax import lax
from jax.experimental import pallas as pl
from jax.experimental.pallas import tpu as pltpu
from jax.sharding import PartitionSpec as P

BF = jnp.bfloat16
F32 = jnp.float32
MESH = pl.DeviceIdType.MESH
NT = (((1,), (1,)), ((), ()))
STRIP = 16
WIDE = 8
PIECES = 2 * WIDE
AHEAD = 3
LAG2 = 3
LAG3 = 6
LAG = 7
TILE = 256
MASK0 = 0b0010100101001010
MASK1 = 0b0100101001010010
B, F, Z, X2, ZB, ZF, ZX2 = range(7)


def kernel(
    q_hbm, s_hbm, scale_hbm, qinv_ref, tinv_ref, o_ref,
    qbuf, g, st, sc, acc, sums, got,
    in_sem, st_sem, ici_sem, sib_sem, own_sem, out_sem, own_out, rs_sem, rs_out,
):
    rows, width = g.shape
    piece_w = width // WIDE
    e = lax.axis_index("example")
    p = lax.axis_index("proj")
    c = lax.rem(e, 2)
    zh = lax.rem(e // 2, 2)
    x = e // 4
    y = lax.rem(p, 4)
    zl = p // 4
    fdir = 1 - 2 * c
    mask = jnp.where(c == 0, MASK0, MASK1)
    xf = lax.rem(x + fdir + 4, 4)
    xb = lax.rem(x - fdir + 4, 4)
    x2 = lax.rem(x + 2, 4)
    zo = 1 - zh

    def at(x_, zh_, c_):
        return {"example": x_ * 4 + zh_ * 2 + c_, "proj": p}

    sib = at(x, zh, 1 - c)
    front = at(xf, zh, c)
    back = at(xb, zh, c)
    across = at(x, zo, c)
    owners = []
    for dz in range(2):
        for dy in range(4):
            if dz or dy:
                y_, zl_ = lax.rem(y + dy, 4), lax.rem(zl + dz, 2)
                owners.append((dz * 4 + dy - 1, zl_ * 4 + y_))

    def strip_row(h, x_, zh_, c_):
        return h * 256 + (x_ * 2 + zh_) * 32 + c_ * STRIP

    own_refs = [
        qbuf.at[pl.ds(pl.multiple_of(strip_row(h, x, zh, c), STRIP), STRIP), :]
        for h in range(2)
    ]
    own_in = [
        pltpu.make_async_copy(q_hbm.at[pl.ds(h * STRIP, STRIP), :], own_refs[h], in_sem.at[h])
        for h in range(2)
    ]
    scale_in = pltpu.make_async_copy(scale_hbm, sc, in_sem.at[2])

    def chunk_in(j):
        slot = lax.rem(j, 2)
        cols = pl.ds(pl.multiple_of(j * piece_w, piece_w), piece_w)
        return pltpu.make_async_copy(s_hbm.at[:, cols], st.at[slot], st_sem.at[slot])

    own_in[0].start()
    own_in[1].start()
    scale_in.start()
    chunk_in(0).start()
    chunk_in(1).start()

    barrier = pltpu.get_barrier_semaphore()
    for target in (sib, front, back, across):
        pl.semaphore_signal(barrier, inc=1, device_id=target, device_id_type=MESH)
    for _, owner in owners:
        pl.semaphore_signal(
            barrier, inc=1, device_id={"example": e, "proj": owner}, device_id_type=MESH
        )
    pl.semaphore_wait(barrier, 4 + len(owners))

    def place(n, x_, zh_):
        late = jnp.where(n >= WIDE, 1, 0)
        row = late * 256 + (x_ * 64 + zh_ * 32 + c * STRIP)
        col = (n - late * WIDE) * piece_w
        return qbuf.at[
            pl.ds(pl.multiple_of(row, STRIP), STRIP),
            pl.ds(pl.multiple_of(col, piece_w), piece_w),
        ]

    def send(n, x_, zh_, target, recv):
        ref = place(n, x_, zh_)
        pltpu.make_async_remote_copy(
            ref, ref, out_sem.at[n], recv, device_id=target, device_id_type=MESH
        ).start()

    def arrived(n, x_, zh_, slot):
        ref = place(n, x_, zh_)
        pltpu.make_async_copy(ref, ref, ici_sem.at[n, slot]).wait()

    def spread_along_z(n):
        return (lax.shift_right_logical(mask, n) & 1) == 1

    def send_own(n):
        send(n, x, zh, across, ici_sem.at[n, Z])
        send(n, x, zh, front, ici_sem.at[n, B])
        send(n, x, zh, back, ici_sem.at[n, F])

    def stage1(n):
        along_z = spread_along_z(n)
        arrived(n, xb, zh, B)
        send(n, xb, zh, front, ici_sem.at[n, X2])

        @pl.when(along_z)
        def _():
            send(n, xb, zh, across, ici_sem.at[n, ZB])

        send(n, xb, zh, sib, sib_sem.at[n])
        arrived(n, x, zo, Z)

        @pl.when(jnp.logical_not(along_z))
        def _():
            send(n, x, zo, front, ici_sem.at[n, ZB])
            send(n, x, zo, back, ici_sem.at[n, ZF])

        send(n, x, zo, sib, sib_sem.at[n])
        arrived(n, xf, zh, F)

        @pl.when(along_z)
        def _():
            send(n, xf, zh, across, ici_sem.at[n, ZF])

        send(n, xf, zh, sib, sib_sem.at[n])

    def stage2(n):
        along_z = spread_along_z(n)
        arrived(n, xb, zo, ZB)

        @pl.when(jnp.logical_not(along_z))
        def _():
            send(n, xb, zo, front, ici_sem.at[n, ZX2])

        send(n, xb, zo, sib, sib_sem.at[n])
        arrived(n, x2, zh, X2)

        @pl.when(along_z)
        def _():
            send(n, x2, zh, across, ici_sem.at[n, ZX2])

        send(n, x2, zh, sib, sib_sem.at[n])
        arrived(n, xf, zo, ZF)
        send(n, xf, zo, sib, sib_sem.at[n])

    def stage3(n):
        arrived(n, x2, zo, ZX2)
        send(n, x2, zo, sib, sib_sem.at[n])

    def dequant(j):
        slot = lax.rem(j, 2)
        chunk_in(j).wait()
        blocks = piece_w // 128
        s = pltpu.roll(sc[...], lax.rem(128 - j * blocks, 128), 1)
        for r in range(0, rows, 128):
            for b in range(blocks):
                cols = pl.ds(pl.multiple_of(j * piece_w + b * 128, 128), 128)
                part = st[slot, r : r + 128, b * 128 : (b + 1) * 128].astype(F32)
                g[r : r + 128, cols] = (part * s[r : r + 128, b : b + 1]).astype(BF)

        @pl.when(j + 2 < WIDE)
        def _():
            chunk_in(j + 2).start()

    def sibling_done(n):
        pieces = qbuf.at[0 : 7 * STRIP, 0:piece_w]
        pltpu.make_async_copy(pieces, pieces, sib_sem.at[n]).wait()

    def multiply(n):
        sibling_done(n)
        late = jnp.where(n >= WIDE, 1, 0)
        group = pl.ds(pl.multiple_of(late * 256, 256), 256)
        cols = pl.ds(pl.multiple_of((n - late * WIDE) * piece_w, piece_w), piece_w)
        acc[group, :] += lax.dot_general(
            qbuf[group, cols], g[:, cols], NT, preferred_element_type=F32
        )

    def send_sums(k, cols):
        group = pl.ds(256 * k, 256)
        sums[group, cols] = acc[group, cols].astype(BF)
        part = k + cols.start // TILE
        for slot, owner in owners:
            start = pl.multiple_of(256 * k + owner * 32, 32)
            pltpu.make_async_remote_copy(
                sums.at[pl.ds(start, 32), cols],
                got.at[slot, pl.ds(32 * k, 32), cols],
                rs_out.at[part],
                rs_sem.at[part, slot],
                device_id={"example": e, "proj": owner},
                device_id_type=MESH,
            ).start()

    def sums_sent(k, cols):
        ref = sums.at[0 : 7 * 32, cols]
        pltpu.make_async_copy(ref, ref, rs_out.at[k + cols.start // TILE]).wait()

    lane = lax.broadcasted_iota(jnp.int32, (64, qinv_ref.shape[0]), 1)
    row = lax.broadcasted_iota(jnp.int32, (64, qinv_ref.shape[0]), 0)
    qrow = qinv_ref[...].reshape(1, -1)
    qcol = jnp.sum(jnp.where(lane == row + p * 64, qrow, 0.0), axis=1, keepdims=True)
    trow = tinv_ref[...].reshape(1, -1)

    def finish(k, cols):
        start = pl.multiple_of(256 * k + p * 32, 32)
        total = acc[pl.ds(start, 32), cols]
        for slot in range(7):
            ref = got.at[slot, pl.ds(32 * k, 32), cols]
            pltpu.make_async_copy(ref, ref, rs_sem.at[k + cols.start // TILE, slot]).wait()
            total += got[slot, pl.ds(32 * k, 32), cols].astype(F32)
        for here, there in ((0, 16 * k), (16, 32 + 16 * k)):
            o_ref[there : there + 16, cols] = (
                total[here : here + 16, :] * qcol[there : there + 16, :] * trow[:, cols]
            )

    own_in[0].wait()
    own_in[1].wait()
    for h in range(2):
        if h == 1:
            for n in range(AHEAD):
                send_own(n)
        pltpu.make_async_remote_copy(
            own_refs[h], own_refs[h], own_out.at[h], own_sem.at[h],
            device_id=sib, device_id_type=MESH,
        ).start()
    acc[...] = jnp.zeros_like(acc)
    scale_in.wait()
    dequant(0)
    for h in range(2):
        ref = qbuf.at[pl.ds(pl.multiple_of(strip_row(h, x, zh, 1 - c), STRIP), STRIP), :]
        pltpu.make_async_copy(ref, ref, own_sem.at[h]).wait()

    def step(s, carry):
        @pl.when(s + AHEAD < PIECES)
        def _():
            send_own(s + AHEAD)

        @pl.when(s < PIECES)
        def _():
            stage1(s)

        @pl.when(s + 1 < WIDE)
        def _():
            dequant(s + 1)

        @pl.when((s >= LAG2) & (s < PIECES + LAG2))
        def _():
            stage2(s - LAG2)

        @pl.when((s >= LAG3) & (s < PIECES + LAG3))
        def _():
            stage3(s - LAG3)

        @pl.when(s >= LAG)
        def _():
            multiply(s - LAG)

        @pl.when(s == WIDE - 1 + LAG)
        def _():
            send_sums(0, slice(0, rows))

        return carry

    lax.fori_loop(0, PIECES + LAG - 1, step, 0)
    sibling_done(PIECES - 1)
    last = slice(width - piece_w, width)
    tiles = [slice(t, t + TILE) for t in range(0, rows, TILE)]
    for tile in tiles:
        acc[256:512, tile] += lax.dot_general(
            qbuf[256:512, last], g[tile, last], NT, preferred_element_type=F32
        )
        send_sums(1, tile)
    finish(0, slice(0, rows))
    for tile in tiles:
        finish(1, tile)
    for n in range(PIECES):
        pieces = qbuf.at[0 : 14 * STRIP, 0:piece_w]
        pltpu.make_async_copy(pieces, pieces, out_sem.at[n]).wait()
    for h in range(2):
        pltpu.make_async_copy(own_refs[h], own_refs[h], own_out.at[h]).wait()
    sums_sent(0, slice(0, rows))
    for tile in tiles:
        sums_sent(1, tile)


def body(queries, store, block_scale, query_inv, train_inv):
    rows, width = store.shape
    n_query = query_inv.shape[0]
    hbm = pl.BlockSpec(memory_space=pl.ANY)
    vmem = pl.BlockSpec(memory_space=pltpu.VMEM)
    dma = pltpu.SemaphoreType.DMA
    return pl.pallas_call(
        kernel,
        out_shape=jax.ShapeDtypeStruct((n_query // 8, rows), F32),
        in_specs=[hbm, hbm, hbm, vmem, vmem],
        out_specs=vmem,
        scratch_shapes=[
            pltpu.VMEM((n_query, width), BF),
            pltpu.VMEM((rows, width), BF),
            pltpu.VMEM((2, rows, width // WIDE), BF),
            pltpu.VMEM((rows, width // 128), F32),
            pltpu.VMEM((n_query, rows), F32),
            pltpu.VMEM((n_query, rows), BF),
            pltpu.VMEM((7, n_query // 8, rows), BF),
            dma((3,)),
            dma((2,)),
            dma((PIECES, 7)),
            dma((PIECES,)),
            dma((2,)),
            dma((PIECES,)),
            dma((2,)),
            dma((1 + rows // TILE, 7)),
            dma((1 + rows // TILE,)),
        ],
        compiler_params=pltpu.CompilerParams(
            collective_id=0, has_side_effects=True, vmem_limit_bytes=60 << 20
        ),
        cost_estimate=pl.CostEstimate(
            flops=2 * n_query * rows * width,
            bytes_accessed=2 * rows * width,
            transcendentals=0,
        ),
        name="gather_score",
    )(queries, store, block_scale, query_inv, train_inv)


def solution(mesh):
    placed = (P("example", "proj"), P("example", "proj"), P("example", "proj"), P(), P("example"))
    return jax.shard_map(
        body, mesh=mesh, in_specs=placed, out_specs=P("proj", "example"), check_vma=False
    )
```

```python
import functools

import jax
import jax.numpy as jnp
from jax import lax
from jax.experimental import pallas as pl
from jax.experimental.pallas import tpu as pltpu
from jax.sharding import PartitionSpec as P

BF = jnp.bfloat16
F32 = jnp.float32
MESH = pl.DeviceIdType.MESH
NT = (((1,), (1,)), ((), ()))
STRIP = 16
WIDE = 8
PIECES = 2 * WIDE
AHEAD = 4
LAG2 = 3
LAG3 = 6
LAG = 7
TILE = 256
MASK0 = 0b0000101010101010
MASK1 = 0b0000010101010101
B, F, Z, X2, ZB, ZF, ZX2 = range(7)


def kernel(
    q_hbm, s_hbm, scale_hbm, qinv_ref, tinv_ref, o_ref,
    qbuf, g, st, sc, acc, sums, got,
    in_sem, st_sem, ici_sem, sib_sem, own_sem, out_sem, own_out, rs_sem, rs_out,
):
    rows, width = g.shape
    piece_w = width // WIDE
    e = lax.axis_index("example")
    p = lax.axis_index("proj")
    c = lax.rem(e, 2)
    zh = lax.rem(e // 2, 2)
    x = e // 4
    y = lax.rem(p, 4)
    zl = p // 4
    fdir = 1 - 2 * c
    mask = jnp.where(c == 0, MASK0, MASK1)
    xf = lax.rem(x + fdir + 4, 4)
    xb = lax.rem(x - fdir + 4, 4)
    x2 = lax.rem(x + 2, 4)
    zo = 1 - zh

    def at(x_, zh_, c_):
        return {"example": x_ * 4 + zh_ * 2 + c_, "proj": p}

    sib = at(x, zh, 1 - c)
    front = at(xf, zh, c)
    back = at(xb, zh, c)
    across = at(x, zo, c)
    owners = []
    for dz in range(2):
        for dy in range(4):
            if dz or dy:
                y_, zl_ = lax.rem(y + dy, 4), lax.rem(zl + dz, 2)
                owners.append((dz * 4 + dy - 1, zl_ * 4 + y_))

    def strip_row(h, x_, zh_, c_):
        return h * 256 + (x_ * 2 + zh_) * 32 + c_ * STRIP

    own_refs = [
        qbuf.at[pl.ds(pl.multiple_of(strip_row(h, x, zh, c), STRIP), STRIP), :]
        for h in range(2)
    ]
    own_in = [
        pltpu.make_async_copy(q_hbm.at[pl.ds(h * STRIP, STRIP), :], own_refs[h], in_sem.at[h])
        for h in range(2)
    ]
    scale_in = pltpu.make_async_copy(scale_hbm, sc, in_sem.at[2])

    def chunk_in(j):
        slot = lax.rem(j, 2)
        cols = pl.ds(pl.multiple_of(j * piece_w, piece_w), piece_w)
        return pltpu.make_async_copy(s_hbm.at[:, cols], st.at[slot], st_sem.at[slot])

    own_in[0].start()
    own_in[1].start()
    scale_in.start()
    chunk_in(0).start()
    chunk_in(1).start()

    barrier = pltpu.get_barrier_semaphore()
    for target in (sib, front, back, across):
        pl.semaphore_signal(barrier, inc=1, device_id=target, device_id_type=MESH)
    for _, owner in owners:
        pl.semaphore_signal(
            barrier, inc=1, device_id={"example": e, "proj": owner}, device_id_type=MESH
        )
    pl.semaphore_wait(barrier, 4 + len(owners))

    def place(n, x_, zh_):
        late = jnp.where(n >= WIDE, 1, 0)
        row = late * 256 + (x_ * 64 + zh_ * 32 + c * STRIP)
        col = (n - late * WIDE) * piece_w
        return qbuf.at[
            pl.ds(pl.multiple_of(row, STRIP), STRIP),
            pl.ds(pl.multiple_of(col, piece_w), piece_w),
        ]

    def send(n, x_, zh_, target, recv):
        ref = place(n, x_, zh_)
        pltpu.make_async_remote_copy(
            ref, ref, out_sem.at[n], recv, device_id=target, device_id_type=MESH
        ).start()

    def arrived(n, x_, zh_, slot):
        ref = place(n, x_, zh_)
        pltpu.make_async_copy(ref, ref, ici_sem.at[n, slot]).wait()

    def spread_along_z(n):
        return (lax.shift_right_logical(mask, n) & 1) == 1

    def send_own(n):
        send(n, x, zh, across, ici_sem.at[n, Z])
        send(n, x, zh, front, ici_sem.at[n, B])
        send(n, x, zh, back, ici_sem.at[n, F])

    def stage1(n):
        along_z = spread_along_z(n)
        arrived(n, xb, zh, B)
        send(n, xb, zh, front, ici_sem.at[n, X2])

        @pl.when(along_z)
        def _():
            send(n, xb, zh, across, ici_sem.at[n, ZB])

        send(n, xb, zh, sib, sib_sem.at[n])
        arrived(n, x, zo, Z)

        @pl.when(jnp.logical_not(along_z))
        def _():
            send(n, x, zo, front, ici_sem.at[n, ZB])
            send(n, x, zo, back, ici_sem.at[n, ZF])

        send(n, x, zo, sib, sib_sem.at[n])
        arrived(n, xf, zh, F)

        @pl.when(along_z)
        def _():
            send(n, xf, zh, across, ici_sem.at[n, ZF])

        send(n, xf, zh, sib, sib_sem.at[n])

    def stage2(n):
        along_z = spread_along_z(n)
        arrived(n, xb, zo, ZB)

        @pl.when(jnp.logical_not(along_z))
        def _():
            send(n, xb, zo, front, ici_sem.at[n, ZX2])

        send(n, xb, zo, sib, sib_sem.at[n])
        arrived(n, x2, zh, X2)

        @pl.when(along_z)
        def _():
            send(n, x2, zh, across, ici_sem.at[n, ZX2])

        send(n, x2, zh, sib, sib_sem.at[n])
        arrived(n, xf, zo, ZF)
        send(n, xf, zo, sib, sib_sem.at[n])

    def stage3(n):
        arrived(n, x2, zo, ZX2)
        send(n, x2, zo, sib, sib_sem.at[n])

    def dequant(j):
        slot = lax.rem(j, 2)
        chunk_in(j).wait()
        blocks = piece_w // 128
        s = pltpu.roll(sc[...], lax.rem(128 - j * blocks, 128), 1)
        for r in range(0, rows, 128):
            for b in range(blocks):
                cols = pl.ds(pl.multiple_of(j * piece_w + b * 128, 128), 128)
                part = st[slot, r : r + 128, b * 128 : (b + 1) * 128].astype(F32)
                g[r : r + 128, cols] = (part * s[r : r + 128, b : b + 1]).astype(BF)

        @pl.when(j + 2 < WIDE)
        def _():
            chunk_in(j + 2).start()

    def sibling_done(n):
        pieces = qbuf.at[0 : 7 * STRIP, 0:piece_w]
        pltpu.make_async_copy(pieces, pieces, sib_sem.at[n]).wait()

    def multiply(n):
        sibling_done(n)
        late = jnp.where(n >= WIDE, 1, 0)
        group = pl.ds(pl.multiple_of(late * 256, 256), 256)
        cols = pl.ds(pl.multiple_of((n - late * WIDE) * piece_w, piece_w), piece_w)
        acc[group, :] += lax.dot_general(
            qbuf[group, cols], g[:, cols], NT, preferred_element_type=F32
        )

    def send_sums(k, cols):
        group = pl.ds(256 * k, 256)
        sums[group, cols] = acc[group, cols].astype(BF)
        part = k + cols.start // TILE
        for slot, owner in owners:
            start = pl.multiple_of(256 * k + owner * 32, 32)
            pltpu.make_async_remote_copy(
                sums.at[pl.ds(start, 32), cols],
                got.at[slot, pl.ds(32 * k, 32), cols],
                rs_out.at[part],
                rs_sem.at[part, slot],
                device_id={"example": e, "proj": owner},
                device_id_type=MESH,
            ).start()

    def sums_sent(k, cols):
        ref = sums.at[0 : 7 * 32, cols]
        pltpu.make_async_copy(ref, ref, rs_out.at[k + cols.start // TILE]).wait()

    lane = lax.broadcasted_iota(jnp.int32, (64, qinv_ref.shape[0]), 1)
    row = lax.broadcasted_iota(jnp.int32, (64, qinv_ref.shape[0]), 0)
    qrow = qinv_ref[...].reshape(1, -1)
    qcol = jnp.sum(jnp.where(lane == row + p * 64, qrow, 0.0), axis=1, keepdims=True)
    trow = tinv_ref[...].reshape(1, -1)

    def finish(k, cols):
        start = pl.multiple_of(256 * k + p * 32, 32)
        total = acc[pl.ds(start, 32), cols]
        for slot in range(7):
            ref = got.at[slot, pl.ds(32 * k, 32), cols]
            pltpu.make_async_copy(ref, ref, rs_sem.at[k + cols.start // TILE, slot]).wait()
            total += got[slot, pl.ds(32 * k, 32), cols].astype(F32)
        for here, there in ((0, 16 * k), (16, 32 + 16 * k)):
            o_ref[there : there + 16, cols] = (
                total[here : here + 16, :] * qcol[there : there + 16, :] * trow[:, cols]
            )

    own_in[0].wait()
    own_in[1].wait()
    for h in range(2):
        if h == 1:
            for n in range(AHEAD):
                send_own(n)
        pltpu.make_async_remote_copy(
            own_refs[h], own_refs[h], own_out.at[h], own_sem.at[h],
            device_id=sib, device_id_type=MESH,
        ).start()
    acc[...] = jnp.zeros_like(acc)
    scale_in.wait()
    dequant(0)
    for h in range(2):
        ref = qbuf.at[pl.ds(pl.multiple_of(strip_row(h, x, zh, 1 - c), STRIP), STRIP), :]
        pltpu.make_async_copy(ref, ref, own_sem.at[h]).wait()

    def step(s, carry):
        @pl.when(s + AHEAD < PIECES)
        def _():
            send_own(s + AHEAD)

        @pl.when(s < PIECES)
        def _():
            stage1(s)

        @pl.when(s + 1 < WIDE)
        def _():
            dequant(s + 1)

        @pl.when((s >= LAG2) & (s < PIECES + LAG2))
        def _():
            stage2(s - LAG2)

        @pl.when((s >= LAG3) & (s < PIECES + LAG3))
        def _():
            stage3(s - LAG3)

        @pl.when(s >= LAG)
        def _():
            multiply(s - LAG)

        @pl.when(s == WIDE - 1 + LAG)
        def _():
            send_sums(0, slice(0, rows))

        return carry

    lax.fori_loop(0, PIECES + LAG - 1, step, 0)
    sibling_done(PIECES - 1)
    last = slice(width - piece_w, width)
    tiles = [slice(t, t + TILE) for t in range(0, rows, TILE)]
    for tile in tiles:
        acc[256:512, tile] += lax.dot_general(
            qbuf[256:512, last], g[tile, last], NT, preferred_element_type=F32
        )
        send_sums(1, tile)
    finish(0, slice(0, rows))
    for tile in tiles:
        finish(1, tile)
    for n in range(PIECES):
        pieces = qbuf.at[0 : 14 * STRIP, 0:piece_w]
        pltpu.make_async_copy(pieces, pieces, out_sem.at[n]).wait()
    for h in range(2):
        pltpu.make_async_copy(own_refs[h], own_refs[h], own_out.at[h]).wait()
    sums_sent(0, slice(0, rows))
    for tile in tiles:
        sums_sent(1, tile)


def body(queries, store, block_scale, query_inv, train_inv):
    rows, width = store.shape
    n_query = query_inv.shape[0]
    hbm = pl.BlockSpec(memory_space=pl.ANY)
    vmem = pl.BlockSpec(memory_space=pltpu.VMEM)
    dma = pltpu.SemaphoreType.DMA
    return pl.pallas_call(
        kernel,
        out_shape=jax.ShapeDtypeStruct((n_query // 8, rows), F32),
        in_specs=[hbm, hbm, hbm, vmem, vmem],
        out_specs=vmem,
        scratch_shapes=[
            pltpu.VMEM((n_query, width), BF),
            pltpu.VMEM((rows, width), BF),
            pltpu.VMEM((2, rows, width // WIDE), BF),
            pltpu.VMEM((rows, width // 128), F32),
            pltpu.VMEM((n_query, rows), F32),
            pltpu.VMEM((n_query, rows), BF),
            pltpu.VMEM((7, n_query // 8, rows), BF),
            dma((3,)),
            dma((2,)),
            dma((PIECES, 7)),
            dma((PIECES,)),
            dma((2,)),
            dma((PIECES,)),
            dma((2,)),
            dma((1 + rows // TILE, 7)),
            dma((1 + rows // TILE,)),
        ],
        compiler_params=pltpu.CompilerParams(
            collective_id=0, has_side_effects=True, vmem_limit_bytes=60 << 20
        ),
        cost_estimate=pl.CostEstimate(
            flops=2 * n_query * rows * width,
            bytes_accessed=2 * rows * width,
            transcendentals=0,
        ),
        name="gather_score",
    )(queries, store, block_scale, query_inv, train_inv)


def solution(mesh):
    placed = (P("example", "proj"), P("example", "proj"), P("example", "proj"), P(), P("example"))
    return jax.shard_map(
        body, mesh=mesh, in_specs=placed, out_specs=P("proj", "example"), check_vma=False
    )
```

```python
import functools

import jax
import jax.numpy as jnp
from jax import lax
from jax.experimental import pallas as pl
from jax.experimental.pallas import tpu as pltpu
from jax.sharding import PartitionSpec as P

BF = jnp.bfloat16
F32 = jnp.float32
MESH = pl.DeviceIdType.MESH
NT = (((1,), (1,)), ((), ()))
STRIP = 16
WIDE = 8
PIECES = 2 * WIDE
AHEAD = 4
LAG2 = 3
LAG3 = 6
LAG = 7
TILE = 256
MASK0 = 0b0000010101011010
MASK1 = 0b0000001010110101
B, F, Z, X2, ZB, ZF, ZX2 = range(7)


def kernel(
    q_hbm, s_hbm, scale_hbm, qinv_ref, tinv_ref, o_ref,
    qbuf, g, st, sc, acc, sums, got,
    in_sem, st_sem, ici_sem, sib_sem, own_sem, out_sem, own_out, rs_sem, rs_out,
):
    rows, width = g.shape
    piece_w = width // WIDE
    e = lax.axis_index("example")
    p = lax.axis_index("proj")
    c = lax.rem(e, 2)
    zh = lax.rem(e // 2, 2)
    x = e // 4
    y = lax.rem(p, 4)
    zl = p // 4
    fdir = 1 - 2 * c
    mask = jnp.where(c == 0, MASK0, MASK1)
    xf = lax.rem(x + fdir + 4, 4)
    xb = lax.rem(x - fdir + 4, 4)
    x2 = lax.rem(x + 2, 4)
    zo = 1 - zh

    def at(x_, zh_, c_):
        return {"example": x_ * 4 + zh_ * 2 + c_, "proj": p}

    sib = at(x, zh, 1 - c)
    front = at(xf, zh, c)
    back = at(xb, zh, c)
    across = at(x, zo, c)
    owners = []
    for dz in range(2):
        for dy in range(4):
            if dz or dy:
                y_, zl_ = lax.rem(y + dy, 4), lax.rem(zl + dz, 2)
                owners.append((dz * 4 + dy - 1, zl_ * 4 + y_))

    def strip_row(h, x_, zh_, c_):
        return h * 256 + (x_ * 2 + zh_) * 32 + c_ * STRIP

    own_refs = [
        qbuf.at[pl.ds(pl.multiple_of(strip_row(h, x, zh, c), STRIP), STRIP), :]
        for h in range(2)
    ]
    own_in = [
        pltpu.make_async_copy(q_hbm.at[pl.ds(h * STRIP, STRIP), :], own_refs[h], in_sem.at[h])
        for h in range(2)
    ]
    scale_in = pltpu.make_async_copy(scale_hbm, sc, in_sem.at[2])

    def chunk_in(j):
        slot = lax.rem(j, 2)
        cols = pl.ds(pl.multiple_of(j * piece_w, piece_w), piece_w)
        return pltpu.make_async_copy(s_hbm.at[:, cols], st.at[slot], st_sem.at[slot])

    own_in[0].start()
    own_in[1].start()
    scale_in.start()
    chunk_in(0).start()
    chunk_in(1).start()

    barrier = pltpu.get_barrier_semaphore()
    for target in (sib, front, back, across):
        pl.semaphore_signal(barrier, inc=1, device_id=target, device_id_type=MESH)
    for _, owner in owners:
        pl.semaphore_signal(
            barrier, inc=1, device_id={"example": e, "proj": owner}, device_id_type=MESH
        )
    pl.semaphore_wait(barrier, 4 + len(owners))

    def place(n, x_, zh_):
        late = jnp.where(n >= WIDE, 1, 0)
        row = late * 256 + (x_ * 64 + zh_ * 32 + c * STRIP)
        col = (n - late * WIDE) * piece_w
        return qbuf.at[
            pl.ds(pl.multiple_of(row, STRIP), STRIP),
            pl.ds(pl.multiple_of(col, piece_w), piece_w),
        ]

    def send(n, x_, zh_, target, recv):
        ref = place(n, x_, zh_)
        pltpu.make_async_remote_copy(
            ref, ref, out_sem.at[n], recv, device_id=target, device_id_type=MESH
        ).start()

    def arrived(n, x_, zh_, slot):
        ref = place(n, x_, zh_)
        pltpu.make_async_copy(ref, ref, ici_sem.at[n, slot]).wait()

    def spread_along_z(n):
        return (lax.shift_right_logical(mask, n) & 1) == 1

    def send_own(n):
        send(n, x, zh, across, ici_sem.at[n, Z])
        send(n, x, zh, front, ici_sem.at[n, B])
        send(n, x, zh, back, ici_sem.at[n, F])

    def stage1(n):
        along_z = spread_along_z(n)
        arrived(n, xb, zh, B)
        send(n, xb, zh, front, ici_sem.at[n, X2])

        @pl.when(along_z)
        def _():
            send(n, xb, zh, across, ici_sem.at[n, ZB])

        send(n, xb, zh, sib, sib_sem.at[n])
        arrived(n, x, zo, Z)

        @pl.when(jnp.logical_not(along_z))
        def _():
            send(n, x, zo, front, ici_sem.at[n, ZB])
            send(n, x, zo, back, ici_sem.at[n, ZF])

        send(n, x, zo, sib, sib_sem.at[n])
        arrived(n, xf, zh, F)

        @pl.when(along_z)
        def _():
            send(n, xf, zh, across, ici_sem.at[n, ZF])

        send(n, xf, zh, sib, sib_sem.at[n])

    def stage2(n):
        along_z = spread_along_z(n)
        arrived(n, xb, zo, ZB)

        @pl.when(jnp.logical_not(along_z))
        def _():
            send(n, xb, zo, front, ici_sem.at[n, ZX2])

        send(n, xb, zo, sib, sib_sem.at[n])
        arrived(n, x2, zh, X2)

        @pl.when(along_z)
        def _():
            send(n, x2, zh, across, ici_sem.at[n, ZX2])

        send(n, x2, zh, sib, sib_sem.at[n])
        arrived(n, xf, zo, ZF)
        send(n, xf, zo, sib, sib_sem.at[n])

    def stage3(n):
        arrived(n, x2, zo, ZX2)
        send(n, x2, zo, sib, sib_sem.at[n])

    def dequant(j):
        slot = lax.rem(j, 2)
        chunk_in(j).wait()
        blocks = piece_w // 128
        s = pltpu.roll(sc[...], lax.rem(128 - j * blocks, 128), 1)
        for r in range(0, rows, 128):
            for b in range(blocks):
                cols = pl.ds(pl.multiple_of(j * piece_w + b * 128, 128), 128)
                part = st[slot, r : r + 128, b * 128 : (b + 1) * 128].astype(F32)
                g[r : r + 128, cols] = (part * s[r : r + 128, b : b + 1]).astype(BF)

        @pl.when(j + 2 < WIDE)
        def _():
            chunk_in(j + 2).start()

    def sibling_done(n):
        pieces = qbuf.at[0 : 7 * STRIP, 0:piece_w]
        pltpu.make_async_copy(pieces, pieces, sib_sem.at[n]).wait()

    def multiply(n):
        sibling_done(n)
        late = jnp.where(n >= WIDE, 1, 0)
        group = pl.ds(pl.multiple_of(late * 256, 256), 256)
        cols = pl.ds(pl.multiple_of((n - late * WIDE) * piece_w, piece_w), piece_w)
        acc[group, :] += lax.dot_general(
            qbuf[group, cols], g[:, cols], NT, preferred_element_type=F32
        )

    def send_sums(k, cols):
        group = pl.ds(256 * k, 256)
        sums[group, cols] = acc[group, cols].astype(BF)
        part = k + cols.start // TILE
        for slot, owner in owners:
            start = pl.multiple_of(256 * k + owner * 32, 32)
            pltpu.make_async_remote_copy(
                sums.at[pl.ds(start, 32), cols],
                got.at[slot, pl.ds(32 * k, 32), cols],
                rs_out.at[part],
                rs_sem.at[part, slot],
                device_id={"example": e, "proj": owner},
                device_id_type=MESH,
            ).start()

    def sums_sent(k, cols):
        ref = sums.at[0 : 7 * 32, cols]
        pltpu.make_async_copy(ref, ref, rs_out.at[k + cols.start // TILE]).wait()

    lane = lax.broadcasted_iota(jnp.int32, (64, qinv_ref.shape[0]), 1)
    row = lax.broadcasted_iota(jnp.int32, (64, qinv_ref.shape[0]), 0)
    qrow = qinv_ref[...].reshape(1, -1)
    qcol = jnp.sum(jnp.where(lane == row + p * 64, qrow, 0.0), axis=1, keepdims=True)
    trow = tinv_ref[...].reshape(1, -1)

    def finish(k, cols):
        start = pl.multiple_of(256 * k + p * 32, 32)
        total = acc[pl.ds(start, 32), cols]
        for slot in range(7):
            ref = got.at[slot, pl.ds(32 * k, 32), cols]
            pltpu.make_async_copy(ref, ref, rs_sem.at[k + cols.start // TILE, slot]).wait()
            total += got[slot, pl.ds(32 * k, 32), cols].astype(F32)
        for here, there in ((0, 16 * k), (16, 32 + 16 * k)):
            o_ref[there : there + 16, cols] = (
                total[here : here + 16, :] * qcol[there : there + 16, :] * trow[:, cols]
            )

    own_in[0].wait()
    own_in[1].wait()
    for h in range(2):
        if h == 1:
            for n in range(AHEAD):
                send_own(n)
        pltpu.make_async_remote_copy(
            own_refs[h], own_refs[h], own_out.at[h], own_sem.at[h],
            device_id=sib, device_id_type=MESH,
        ).start()
    acc[...] = jnp.zeros_like(acc)
    scale_in.wait()
    dequant(0)
    for h in range(2):
        ref = qbuf.at[pl.ds(pl.multiple_of(strip_row(h, x, zh, 1 - c), STRIP), STRIP), :]
        pltpu.make_async_copy(ref, ref, own_sem.at[h]).wait()

    def step(s, carry):
        @pl.when(s + AHEAD < PIECES)
        def _():
            send_own(s + AHEAD)

        @pl.when(s < PIECES)
        def _():
            stage1(s)

        @pl.when(s + 1 < WIDE)
        def _():
            dequant(s + 1)

        @pl.when((s >= LAG2) & (s < PIECES + LAG2))
        def _():
            stage2(s - LAG2)

        @pl.when((s >= LAG3) & (s < PIECES + LAG3))
        def _():
            stage3(s - LAG3)

        @pl.when(s >= LAG)
        def _():
            multiply(s - LAG)

        @pl.when(s == WIDE - 1 + LAG)
        def _():
            send_sums(0, slice(0, rows))

        return carry

    lax.fori_loop(0, PIECES + LAG - 1, step, 0)
    sibling_done(PIECES - 1)
    last = slice(width - piece_w, width)
    tiles = [slice(t, t + TILE) for t in range(0, rows, TILE)]
    for tile in tiles:
        acc[256:512, tile] += lax.dot_general(
            qbuf[256:512, last], g[tile, last], NT, preferred_element_type=F32
        )
        send_sums(1, tile)
    finish(0, slice(0, rows))
    for tile in tiles:
        finish(1, tile)
    for n in range(PIECES):
        pieces = qbuf.at[0 : 14 * STRIP, 0:piece_w]
        pltpu.make_async_copy(pieces, pieces, out_sem.at[n]).wait()
    for h in range(2):
        pltpu.make_async_copy(own_refs[h], own_refs[h], own_out.at[h]).wait()
    sums_sent(0, slice(0, rows))
    for tile in tiles:
        sums_sent(1, tile)


def body(queries, store, block_scale, query_inv, train_inv):
    rows, width = store.shape
    n_query = query_inv.shape[0]
    hbm = pl.BlockSpec(memory_space=pl.ANY)
    vmem = pl.BlockSpec(memory_space=pltpu.VMEM)
    dma = pltpu.SemaphoreType.DMA
    return pl.pallas_call(
        kernel,
        out_shape=jax.ShapeDtypeStruct((n_query // 8, rows), F32),
        in_specs=[hbm, hbm, hbm, vmem, vmem],
        out_specs=vmem,
        scratch_shapes=[
            pltpu.VMEM((n_query, width), BF),
            pltpu.VMEM((rows, width), BF),
            pltpu.VMEM((2, rows, width // WIDE), BF),
            pltpu.VMEM((rows, width // 128), F32),
            pltpu.VMEM((n_query, rows), F32),
            pltpu.VMEM((n_query, rows), BF),
            pltpu.VMEM((7, n_query // 8, rows), BF),
            dma((3,)),
            dma((2,)),
            dma((PIECES, 7)),
            dma((PIECES,)),
            dma((2,)),
            dma((PIECES,)),
            dma((2,)),
            dma((1 + rows // TILE, 7)),
            dma((1 + rows // TILE,)),
        ],
        compiler_params=pltpu.CompilerParams(
            collective_id=0, has_side_effects=True, vmem_limit_bytes=60 << 20
        ),
        cost_estimate=pl.CostEstimate(
            flops=2 * n_query * rows * width,
            bytes_accessed=2 * rows * width,
            transcendentals=0,
        ),
        name="gather_score",
    )(queries, store, block_scale, query_inv, train_inv)


def solution(mesh):
    placed = (P("example", "proj"), P("example", "proj"), P("example", "proj"), P(), P("example"))
    return jax.shard_map(
        body, mesh=mesh, in_specs=placed, out_specs=P("proj", "example"), check_vma=False
    )
```
